1024 devices in a mesh: user: 64 (over z_lo, y), item: 16 (over z_hi, x, core).
Axes of the slice: x: 4, y: 4, z: 32 (z_hi: 2, z_lo: 16; z = z_hi * 16 + z_lo), core: 2. Of those that a mesh axis runs over, the one named last changes fastest.
Arguments:
- item_features: bfloat16 [65536, 2048], P(('item', 'user')), may hold values from -6 to 6
- layer_one: bfloat16 [2048, 1024], replicated, may hold values from -0.125 to 0.125
- layer_two: bfloat16 [1024, 512], replicated, may hold values from -0.1875 to 0.1875
- log_weight: float32 [65536], P(('item', 'user')), may hold values from 0 to 4.9
- user_vectors: bfloat16 [32768, 512], P('user'), may hold values from -360 to 360
- positive_index: int32 [32768], P('user'), may hold values from 0 to 65535
Outputs:
- row_loss: float32 [32768], P('user')
- col_lse: float32 [65536], P(('item', 'user'))
The draws below stay inside these ranges and needn't reach their ends.
All inputs are finite; a program needn't handle non-finite values.
Results may differ from the reference program's by a relative error of at most 0.007.
Values may be sent and summed in bfloat16 or wider, within the bound.
No kernel may reach another device: no remote copies, remote signals or barrier semaphores. Data moves between devices by JAX's collectives and lax.ppermute only.
A program may use at most 64 MiB of HBM per device.

```python
import math
import jax
import jax.numpy as jnp
from jax import lax

D_IN = 2048
D_HID = 1024
D_EMB = 512
ITEM_DEV = 64
ITEMS = 65536
USERS = 32768
N_USER = 64


def draw_user_vectors(key, part):
    key = jax.random.fold_in(key, 11)
    first = jax.random.fold_in(key, 0)
    base = jnp.clip(jax.random.normal(first, (USERS, D_EMB), jnp.float32), -6.0, 6.0)
    return base.astype(jnp.bfloat16)


def draw_positive_index(key, part):
    key = jax.random.fold_in(key, 23)
    first, second, third = jax.random.split(key, 3)
    chosen = jax.random.randint(first, (USERS,), 0, ITEMS, jnp.int32)
    low_spot = jax.random.randint(second, (), 0, USERS // 2, jnp.int32)
    high_spot = jax.random.randint(third, (), USERS // 2, USERS, jnp.int32)
    chosen = chosen.at[low_spot].set(0)
    chosen = chosen.at[high_spot].set(ITEMS - 1)
    return chosen


def ramped_weight(key, height):
    rough = jax.random.uniform(key, (ITEMS,), jnp.float32, 0.0, 1.5)
    place = jnp.arange(ITEMS, dtype=jnp.float32) / float(ITEMS)
    return rough + height * place


def draw_log_weight(key, part):
    key = jax.random.fold_in(key, 37)
    return ramped_weight(key, math.log(10.0))


def block_scale(rng, dims, cuts, smallest, largest):
    level = 1.0
    for dim, shards_of in cuts:
        heights = jax.random.uniform(jax.random.fold_in(jax.random.fold_in(rng, 6), dim), (shards_of,), jnp.float32, smallest / len(cuts), largest / len(cuts))
        level = level * jnp.repeat(jnp.exp(heights), dims[dim] // shards_of).reshape((-1,) + (1,) * (len(dims) - 1 - dim))
    return level


def noise(own_key, dims, scale, most, pieces=(), kind=jnp.bfloat16):
    values = jax.random.normal(own_key, dims, jnp.float32) * scale
    if len(pieces) > 0:
        values = block_scale(own_key, dims, pieces, -0.22, 0.18) * values
    return jnp.clip(values, min=-most, max=most).astype(kind)


def setup_inputs(seed: int = 0) -> dict:
    key_list = jax.random.split(jax.random.key(seed), 7)
    item_features = noise(key_list[0], (ITEMS, D_IN), 1.0, 6.0, ((0, 1024),))
    layer_one = noise(key_list[1], (D_IN, D_HID), D_IN ** -0.5, 0.125)
    layer_two = noise(key_list[2], (D_HID, D_EMB), D_HID ** -0.5, 0.1875)
    log_weight = draw_log_weight(jax.random.fold_in(key_list[6], 71), 0)
    user_vectors = draw_user_vectors(jax.random.fold_in(key_list[6], 71), 0)
    positive_index = draw_positive_index(jax.random.fold_in(key_list[6], 71), 0)
    return dict(item_features=item_features, layer_one=layer_one, layer_two=layer_two, log_weight=log_weight, user_vectors=user_vectors, positive_index=positive_index)


def reference(item_features, layer_one, layer_two, log_weight, user_vectors, positive_index):
    hidden = jax.nn.relu(jnp.dot(item_features, layer_one, preferred_element_type=jnp.float32)).astype(jnp.bfloat16)
    embedded = jnp.dot(hidden, layer_two, preferred_element_type=jnp.float32).astype(jnp.bfloat16)
    block = ITEM_DEV * N_USER
    count = ITEMS // block
    inverse_temp = 4.0 / math.sqrt(D_EMB)
    vectors = embedded.reshape(count, block, D_EMB)
    weights = log_weight.reshape(count, block)
    indices = jnp.arange(count, dtype=jnp.int32)

    def step(carry, inputs):
        row_max, row_sum, row_positive = carry
        piece, piece_weight, index = inputs
        scores = jnp.dot(user_vectors, piece.T, preferred_element_type=jnp.float32) * inverse_temp
        top_col = lax.optimization_barrier(jnp.max(scores, axis=0))
        lse_col = top_col + jnp.log(lax.optimization_barrier(jnp.sum(jnp.exp(scores - top_col[None, :]), axis=0)))
        logits = scores + piece_weight[None, :]
        new_max = jnp.maximum(row_max, lax.optimization_barrier(jnp.max(logits, axis=1)))
        row_sum = row_sum * jnp.exp(row_max - new_max) + lax.optimization_barrier(jnp.sum(jnp.exp(logits - new_max[:, None]), axis=1))
        columns = index * block + jnp.arange(block, dtype=jnp.int32)
        hits = positive_index[:, None] == columns[None, :]
        row_positive = row_positive + lax.optimization_barrier(jnp.sum(jnp.where(hits, logits, jnp.zeros_like(logits)), axis=1))
        return ((new_max, row_sum, row_positive), lse_col)
    start = (jnp.full((USERS,), -1e+30, jnp.float32), jnp.zeros((USERS,), jnp.float32), jnp.zeros((USERS,), jnp.float32))
    carry, columns_lse = lax.scan(step, start, (vectors, weights, indices))
    row_max, row_sum, row_positive = carry
    row_loss = row_max + jnp.log(row_sum) - row_positive
    return (row_loss, columns_lse.reshape(ITEMS))
```

```python
import functools
import math

import jax
import jax.numpy as jnp
from jax import lax
from jax.experimental import pallas as pl
from jax.experimental.pallas import tpu as pltpu
from jax.sharding import Mesh
from jax.sharding import PartitionSpec as P

F32, BF16 = jnp.float32, jnp.bfloat16
AXES = ("zl", "y", "zh", "x", "c")
SIZES = (16, 4, 2, 4, 2)
ZC = ("zl", "zh", "c")
PLANE = ("y", "x", "c")
RING = 32
BLOCK = 64
USERS = 512
Y = 4
DEPTH = 512
ITEMS = 256
EXTRA = 16
TEMP = 4.0 / math.sqrt(DEPTH)
LOG2E = 1.0 / math.log(2.0)
CHUNK = 32


def ring_index(z, c):
    z = z % RING
    return (z % 16 * 2 + z // 16) * 2 + c


def along(distance):
    return [
        (ring_index(z, c), ring_index(z + (distance if c == 0 else -distance), c))
        for z in range(RING)
        for c in range(2)
    ]


def across(distance):
    return [
        (ring_index(z, c), ring_index(z + (distance if c == 1 else -distance), 1 - c))
        for z in range(RING)
        for c in range(2)
    ]


def high_low(values):
    high = values.astype(BF16)
    return high, (values - high.astype(F32)).astype(BF16)


def score_kernel(first, last, base_ref, items_ref, users_ref, *refs):
    if first:
        item_ref, row_ref, scores, weight, ids, top_item, sum_item = refs
    else:
        past_ref, item_ref, row_ref, scores, weight, ids, top_item, sum_item = refs
    extra = items_ref[ITEMS : ITEMS + EXTRA, 0:256].astype(F32)
    packed = (extra[:, 0:128] + extra[:, 128:256]) * (1.0 / TEMP)
    for half in range(2):
        row = packed[8 * half : 8 * half + 1, :]
        weight[128 * half : 128 * half + 128, :] = jnp.broadcast_to(row, (128, 128)).T
    spot = lax.broadcasted_iota(jnp.int32, (BLOCK, 128), 0)
    for part in range(ITEMS // BLOCK):
        ids[part * BLOCK : (part + 1) * BLOCK, :] = (spot + base_ref[part]).astype(F32)

    chunks = [slice(g, g + CHUNK) for g in range(0, ITEMS, CHUNK)]
    tiles = [slice(k, k + 128) for k in range(0, USERS, 128)]
    tops, positives = [], []
    for y in range(Y):
        start = y * (USERS + EXTRA)
        raw = lax.dot_general(
            items_ref[0:ITEMS, :],
            users_ref[start : start + USERS, :],
            (((1,), (1,)), ((), ())),
            preferred_element_type=F32,
        )
        index_rows = users_ref[start + USERS : start + USERS + EXTRA, :].astype(F32)
        wanted = index_rows[0:1, :] * 256.0 + index_rows[1:2, :]
        top_y, positive_y = [], []
        for k in tiles:
            top, positive = None, None
            for g in chunks:
                piece = raw[g, k]
                scores[g, y * USERS + k.start : y * USERS + k.stop] = piece
                if y == 0 and k.start == 0:
                    top_item[g, :] = piece
                else:
                    top_item[g, :] = jnp.maximum(top_item[g, :], piece)
                logits = piece + weight[g, :]
                found = jnp.where(ids[g, :] == wanted[:, k], logits, 0.0)
                shape = (CHUNK // 8, 8, 128)
                part_top = jnp.max(logits.reshape(shape), axis=0)
                part_positive = jnp.sum(found.reshape(shape), axis=0)
                top = part_top if top is None else jnp.maximum(top, part_top)
                positive = part_positive if positive is None else positive + part_positive
            top_y.append(jnp.max(top, axis=0, keepdims=True))
            positive_y.append(jnp.sum(positive, axis=0, keepdims=True))
        tops.append(top_y)
        positives.append(positive_y)

    for g in chunks:
        top_item[g, :] = jnp.broadcast_to(
            jnp.max(top_item[g, :], axis=1, keepdims=True), (CHUNK, 128)
        )
    for y in range(Y):
        for t, k in enumerate(tiles):
            place = slice(y * USERS + k.start, y * USERS + k.stop)
            top, positive = tops[y][t], positives[y][t]
            if not first:
                old_top = past_ref[0:1, place]
                top = jnp.maximum(old_top, top)
                positive = positive + past_ref[2:3, place]
            total = None
            for g in chunks:
                piece = scores[g, place]
                by_item = jnp.exp2((piece - top_item[g, :]) * (TEMP * LOG2E))
                if y == 0 and t == 0:
                    sum_item[g, :] = by_item
                else:
                    sum_item[g, :] = sum_item[g, :] + by_item
                by_user = jnp.exp2((piece + weight[g, :] - top) * (TEMP * LOG2E))
                part = jnp.sum(by_user.reshape(CHUNK // 8, 8, 128), axis=0)
                total = part if total is None else total + part
            total = jnp.sum(total, axis=0, keepdims=True)
            if not first:
                total = total + past_ref[1:2, place] * jnp.exp2((old_top - top) * (TEMP * LOG2E))
            if last:
                lse = top * TEMP + jnp.log(total)
                for peer in range(8):
                    tile = (y * 8 + peer) * 8
                    row_ref[tile + t : tile + t + 1, :] = lse
                    row_ref[tile + 4 + t : tile + 5 + t, :] = positive * TEMP
            else:
                row_ref[0:1, place] = top
                row_ref[1:2, place] = total
                row_ref[2:3, place] = positive
    for half in range(2):
        g = slice(128 * half, 128 * half + 128)
        total = jnp.broadcast_to(jnp.sum(sum_item[g, :], axis=1, keepdims=True), (128, 128))
        lse = top_item[g, :] * TEMP + jnp.log(total)
        item_ref[0:1, g] = lse.T[0:1, :]


def score_call(first, last, bases, items, users, past):
    vmem = pl.BlockSpec(memory_space=pltpu.VMEM)
    operands = (bases, items, users) + (() if first else (past,))
    row_shape = (32 * 8, 128) if last else (8, Y * USERS)
    return pl.pallas_call(
        functools.partial(score_kernel, first, last),
        out_shape=(
            jax.ShapeDtypeStruct((1, ITEMS), F32),
            jax.ShapeDtypeStruct(row_shape, F32),
        ),
        in_specs=[pl.BlockSpec(memory_space=pltpu.SMEM)] + [vmem] * (len(operands) - 1),
        out_specs=(vmem, vmem),
        scratch_shapes=[
            pltpu.VMEM((ITEMS, Y * USERS), F32),
            pltpu.VMEM((ITEMS, 128), F32),
            pltpu.VMEM((ITEMS, 128), F32),
            pltpu.VMEM((ITEMS, 128), F32),
            pltpu.VMEM((ITEMS, 128), F32),
        ],
        compiler_params=pltpu.CompilerParams(vmem_limit_bytes=24 * 1024 * 1024),
        cost_estimate=pl.CostEstimate(
            flops=2 * ITEMS * Y * USERS * DEPTH,
            bytes_accessed=4 * 1024 * 1024,
            transcendentals=2 * ITEMS * Y * USERS,
        ),
    )(*operands)


def join(*parts):
    top = functools.reduce(jnp.maximum, parts)
    return top + jnp.log(sum(jnp.exp(part - top) for part in parts))


def on_device(item_features, layer_one, layer_two, log_weight, user_vectors, positive_index):
    high = (positive_index // 256).astype(BF16)
    low = (positive_index % 256).astype(BF16)
    index_rows = jnp.pad(jnp.stack([high, low]), ((0, EXTRA - 2), (0, 0)))
    users = lax.all_gather(
        jnp.concatenate([user_vectors, index_rows], axis=0), "y", axis=0, tiled=True
    )

    hidden = jax.nn.relu(
        jnp.dot(item_features, layer_one, preferred_element_type=F32)
    ).astype(BF16)
    embedded = jnp.dot(hidden, layer_two, preferred_element_type=F32).astype(BF16)
    weight_high, weight_low = high_low(log_weight)

    def rows(values):
        return jnp.pad(values[None, :], ((0, 7), (0, DEPTH - values.shape[0])))

    sent = jnp.concatenate([embedded, rows(jnp.concatenate([weight_high, weight_low]))], axis=0)
    came = lax.ppermute(sent, ZC, across(1))
    weights = jnp.concatenate(
        [weight_high, came[BLOCK, 0:BLOCK], weight_low, came[BLOCK, BLOCK : 2 * BLOCK]]
    )
    near = jnp.concatenate([embedded, came[0:BLOCK], rows(weights)], axis=0)
    far = lax.ppermute(near, ZC, along(4))
    pair = jnp.concatenate(
        [near[: 2 * BLOCK], far[: 2 * BLOCK], near[2 * BLOCK :], far[2 * BLOCK :]], axis=0
    )

    zl, y, zh, x, c = (lax.axis_index(name) for name in AXES)
    z = zh * 16 + zl

    def base(place, core):
        place = place % RING
        item = ((place // 16) * 4 + x) * 2 + core
        return (item * 64 + (place % 16) * 4 + y) * BLOCK

    side = jnp.where(c == 0, -1, 1)
    columns, past = [], None
    for step in range(4):
        ahead = lax.ppermute(pair, ZC, along(1)) if step < 3 else None
        bases = jnp.stack(
            [
                base(z + side * (step + more + cross), jnp.where(cross == 0, c, 1 - c))
                for more in (0, 4)
                for cross in (0, 1)
            ]
        ).astype(jnp.int32)
        column, past = score_call(step == 0, step == 3, bases, pair, users, past)
        columns.append(column)
        pair = ahead

    stacked = jnp.concatenate(columns, axis=0)
    came4 = lax.ppermute(stacked[:, 128:], ZC, along(-4))
    four = join(stacked[:, :128], came4)
    came2 = lax.ppermute(four[2:], ZC, along(-2))
    two = join(four[:2], came2)
    one_away = lax.ppermute(two[1, :BLOCK], ZC, along(-1))
    cross_one = lax.ppermute(two[0, BLOCK:], ZC, across(1))
    cross_two = lax.ppermute(two[1, BLOCK:], ZC, across(2))

    plane = lax.all_to_all(past, PLANE, 0, 0, tiled=True).reshape(32, 8, 128)
    lse, positive = plane[:, :4], plane[:, 4:]
    top = jnp.max(lse, axis=0)
    lse = top + jnp.log(jnp.sum(jnp.exp(lse - top), axis=0))
    mine = jnp.concatenate([lse, jnp.sum(positive, axis=0)], axis=0)
    other = lax.ppermute(mine, "zh", [(0, 1), (1, 0)])
    row_loss = join(mine[:4], other[:4]) - (mine[4:] + other[4:])

    col_lse = join(two[0, :BLOCK], one_away, cross_one, cross_two)
    return row_loss.reshape(USERS), col_lse


def solution(mesh):
    fine = Mesh(mesh.devices.reshape(SIZES), AXES)
    by_item = ("zh", "x", "c", "zl", "y")
    by_user = ("zl", "y")
    placed = (P(by_item, None), P(), P(), P(by_item), P(by_user, None), P(by_user))
    return jax.shard_map(
        on_device,
        mesh=fine,
        in_specs=placed,
        out_specs=(P(by_user), P(by_item)),
        check_vma=False,
    )
```

```python
import functools
import math

import jax
import jax.numpy as jnp
from jax import lax
from jax.experimental import pallas as pl
from jax.experimental.pallas import tpu as pltpu
from jax.sharding import Mesh
from jax.sharding import PartitionSpec as P

F32, BF16 = jnp.float32, jnp.bfloat16
AXES = ("zl", "y", "zh", "x", "c")
SIZES = (16, 4, 2, 4, 2)
ZC = ("zl", "zh", "c")
PLANE = ("y", "x", "c")
RING = 32
BLOCK = 64
USERS = 512
Y = 4
DEPTH = 512
ITEMS = 256
HALF = ITEMS // 2
EXTRA = 16
TEMP = 4.0 / math.sqrt(DEPTH)
LOG2E = 1.0 / math.log(2.0)
CHUNK = 32


def ring_index(z, c):
    z = z % RING
    return (z % 16 * 2 + z // 16) * 2 + c


def along(distance):
    return [
        (ring_index(z, c), ring_index(z + (distance if c == 0 else -distance), c))
        for z in range(RING)
        for c in range(2)
    ]


def across(distance):
    return [
        (ring_index(z, c), ring_index(z + (distance if c == 1 else -distance), 1 - c))
        for z in range(RING)
        for c in range(2)
    ]


def high_low(values):
    high = values.astype(BF16)
    return high, (values - high.astype(F32)).astype(BF16)


def score_kernel(first, last, base_ref, items_ref, *refs):
    users_refs, refs = refs[:Y], refs[Y:]
    if first:
        item_ref, row_ref, scores, weight, ids, top_item, sum_item = refs
    else:
        past_ref, item_ref, row_ref, scores, weight, ids, top_item, sum_item = refs
    for half in range(2):
        start = half * (HALF + EXTRA) + HALF
        extra = items_ref[start : start + EXTRA, 0:256].astype(F32)
        row = (extra[0:1, 0:128] + extra[0:1, 128:256]) * (1.0 / TEMP)
        weight[HALF * half : HALF * (half + 1), :] = jnp.broadcast_to(row, (HALF, 128)).T
    spot = lax.broadcasted_iota(jnp.int32, (BLOCK, 128), 0)
    for part in range(ITEMS // BLOCK):
        ids[part * BLOCK : (part + 1) * BLOCK, :] = (spot + base_ref[part]).astype(F32)

    chunks = [slice(g, g + CHUNK) for g in range(0, ITEMS, CHUNK)]
    tiles = [slice(k, k + 128) for k in range(0, USERS, 128)]
    items = jnp.concatenate(
        [items_ref[0:HALF, :], items_ref[HALF + EXTRA : 2 * HALF + EXTRA, :]], axis=0
    )
    tops, positives = [], []
    for y in range(Y):
        raw = lax.dot_general(
            items,
            users_refs[y][0:USERS, :],
            (((1,), (1,)), ((), ())),
            preferred_element_type=F32,
        )
        index_rows = users_refs[y][USERS : USERS + EXTRA, :].astype(F32)
        wanted = index_rows[0:1, :] * 256.0 + index_rows[1:2, :]
        top_y, positive_y = [], []
        for k in tiles:
            top, positive = None, None
            for g in chunks:
                piece = raw[g, k]
                scores[g, y * USERS + k.start : y * USERS + k.stop] = piece
                if y == 0 and k.start == 0:
                    top_item[g, :] = piece
                else:
                    top_item[g, :] = jnp.maximum(top_item[g, :], piece)
                logits = piece + weight[g, :]
                found = jnp.where(ids[g, :] == wanted[:, k], logits, 0.0)
                shape = (CHUNK // 8, 8, 128)
                part_top = jnp.max(logits.reshape(shape), axis=0)
                part_positive = jnp.sum(found.reshape(shape), axis=0)
                top = part_top if top is None else jnp.maximum(top, part_top)
                positive = part_positive if positive is None else positive + part_positive
            top_y.append(jnp.max(top, axis=0, keepdims=True))
            positive_y.append(jnp.sum(positive, axis=0, keepdims=True))
        tops.append(top_y)
        positives.append(positive_y)

    for g in chunks:
        top_item[g, :] = jnp.broadcast_to(
            jnp.max(top_item[g, :], axis=1, keepdims=True), (CHUNK, 128)
        )
    for y in range(Y):
        ready = []
        for t, k in enumerate(tiles):
            place = slice(y * USERS + k.start, y * USERS + k.stop)
            top, positive = tops[y][t], positives[y][t]
            if not first:
                old_top = past_ref[0:1, place]
                top = jnp.maximum(old_top, top)
                positive = positive + past_ref[2:3, place]
            total = None
            for g in chunks:
                piece = scores[g, place]
                by_item = jnp.exp2((piece - top_item[g, :]) * (TEMP * LOG2E))
                if y == 0 and t == 0:
                    sum_item[g, :] = by_item
                else:
                    sum_item[g, :] = sum_item[g, :] + by_item
                by_user = jnp.exp2((piece + weight[g, :] - top) * (TEMP * LOG2E))
                part = jnp.sum(by_user.reshape(CHUNK // 8, 8, 128), axis=0)
                total = part if total is None else total + part
            total = jnp.sum(total, axis=0, keepdims=True)
            if not first:
                total = total + past_ref[1:2, place] * jnp.exp2((old_top - top) * (TEMP * LOG2E))
            if last:
                lse = top * TEMP + jnp.log(total)
                ready.append((lse, positive * TEMP))
            else:
                row_ref[0:1, place] = top
                row_ref[1:2, place] = total
                row_ref[2:3, place] = positive
        if last:
            tile = jnp.concatenate([lse for lse, _ in ready] + [pos for _, pos in ready], axis=0)
            block = (base_ref[4] + y) % Y
            for peer in range(8):
                row_ref[pl.ds(pl.multiple_of((block * 8 + peer) * 8, 8), 8), :] = tile
    for half in range(2):
        g = slice(128 * half, 128 * half + 128)
        total = jnp.broadcast_to(jnp.sum(sum_item[g, :], axis=1, keepdims=True), (128, 128))
        lse = top_item[g, :] * TEMP + jnp.log(total)
        item_ref[0:1, g] = lse.T[0:1, :]


def score_call(first, last, bases, items, users, past):
    vmem = pl.BlockSpec(memory_space=pltpu.VMEM)
    operands = (bases, items, *users) + (() if first else (past,))
    row_shape = (32 * 8, 128) if last else (8, Y * USERS)
    return pl.pallas_call(
        functools.partial(score_kernel, first, last),
        out_shape=(
            jax.ShapeDtypeStruct((1, ITEMS), F32),
            jax.ShapeDtypeStruct(row_shape, F32),
        ),
        in_specs=[pl.BlockSpec(memory_space=pltpu.SMEM)] + [vmem] * (len(operands) - 1),
        out_specs=(vmem, vmem),
        scratch_shapes=[
            pltpu.VMEM((ITEMS, Y * USERS), F32),
            pltpu.VMEM((ITEMS, 128), F32),
            pltpu.VMEM((ITEMS, 128), F32),
            pltpu.VMEM((ITEMS, 128), F32),
            pltpu.VMEM((ITEMS, 128), F32),
        ],
        compiler_params=pltpu.CompilerParams(vmem_limit_bytes=24 * 1024 * 1024),
        cost_estimate=pl.CostEstimate(
            flops=2 * ITEMS * Y * USERS * DEPTH,
            bytes_accessed=4 * 1024 * 1024,
            transcendentals=2 * ITEMS * Y * USERS,
        ),
    )(*operands)


def stack_kernel(near_ref, far_ref, pair_ref):
    pair_ref[0 : HALF + EXTRA, :] = near_ref[...]
    pair_ref[HALF + EXTRA :, :] = far_ref[...]


def stack_call(near, far):
    vmem = pl.BlockSpec(memory_space=pltpu.VMEM)
    return pl.pallas_call(
        stack_kernel,
        out_shape=jax.ShapeDtypeStruct((2 * (HALF + EXTRA), DEPTH), BF16),
        in_specs=[vmem, vmem],
        out_specs=vmem,
        cost_estimate=pl.CostEstimate(flops=60 * 10**9, bytes_accessed=600_000, transcendentals=0),
    )(near, far)


def join(*parts):
    top = functools.reduce(jnp.maximum, parts)
    return top + jnp.log(sum(jnp.exp(part - top) for part in parts))


def on_device(item_features, layer_one, layer_two, log_weight, user_vectors, positive_index):
    hidden = jax.nn.relu(
        jnp.dot(item_features, layer_one, preferred_element_type=F32)
    ).astype(BF16)
    embedded = jnp.dot(hidden, layer_two, preferred_element_type=F32).astype(BF16)
    weight_high, weight_low = high_low(log_weight)

    def rows(values, count):
        return jnp.pad(values[None, :], ((0, count - 1), (0, DEPTH - values.shape[0])))

    sent = jnp.concatenate(
        [embedded, rows(jnp.concatenate([weight_high, weight_low]), 8)], axis=0
    )
    came = lax.ppermute(sent, ZC, across(1))
    weights = jnp.concatenate(
        [weight_high, came[BLOCK, 0:BLOCK], weight_low, came[BLOCK, BLOCK : 2 * BLOCK]]
    )
    near = jnp.concatenate([embedded, came[0:BLOCK], rows(weights, EXTRA)], axis=0)

    high = (positive_index // 256).astype(BF16)
    low = (positive_index % 256).astype(BF16)
    index_rows = jnp.pad(jnp.stack([high, low]), ((0, EXTRA - 2), (0, 0)))
    own = jnp.concatenate([user_vectors, index_rows], axis=0)

    far = lax.ppermute(near, ZC, along(4))
    own, near = lax.optimization_barrier((own, near))
    users = [own] + [
        lax.ppermute(own, "y", [(k, (k - r) % Y) for k in range(Y)]) for r in (1, 3, 2)
    ]
    users = [users[0], users[1], users[3], users[2]]
    pair = stack_call(near, far)
    pairs = [pair] + [lax.ppermute(pair, ZC, along(step)) for step in (1, 2, 3)]

    zl, y, zh, x, c = (lax.axis_index(name) for name in AXES)
    z = zh * 16 + zl

    def base(place, core):
        place = place % RING
        item = ((place // 16) * 4 + x) * 2 + core
        return (item * 64 + (place % 16) * 4 + y) * BLOCK

    side = jnp.where(c == 0, -1, 1)
    columns, past = [], None
    for step in range(4):
        bases = jnp.stack(
            [
                base(z + side * (step + more + cross), jnp.where(cross == 0, c, 1 - c))
                for more in (0, 4)
                for cross in (0, 1)
            ]
            + [y]
        ).astype(jnp.int32)
        column, past = score_call(step == 0, step == 3, bases, pairs[step], users, past)
        columns.append(column)

    stacked = jnp.concatenate(columns, axis=0)
    plane = lax.all_to_all(past, PLANE, 0, 0, tiled=True).reshape(32, 8, 128)
    came4 = lax.ppermute(stacked[:, HALF:], ZC, along(-4))

    lse, positive = plane[:, :4], plane[:, 4:]
    top = jnp.max(lse, axis=0)
    lse = top + jnp.log(jnp.sum(jnp.exp(lse - top), axis=0))
    mine = jnp.concatenate([lse, jnp.sum(positive, axis=0)], axis=0)
    came4, mine = lax.optimization_barrier((came4, mine))
    four = join(stacked[:, :HALF], came4)
    other = lax.ppermute(mine, "zh", [(0, 1), (1, 0)])
    came2 = lax.ppermute(four[2:], ZC, along(-2))
    two = join(four[:2], came2)
    one_away = lax.ppermute(two[1, :BLOCK], ZC, along(-1))
    cross_one = lax.ppermute(two[0, BLOCK:], ZC, across(1))
    cross_two = lax.ppermute(two[1, BLOCK:], ZC, across(2))
    row_loss = join(mine[:4], other[:4]) - (mine[4:] + other[4:])
    one_away, row_loss = lax.optimization_barrier((one_away, row_loss))
    col_lse = join(two[0, :BLOCK], one_away, cross_one, cross_two)
    return row_loss.reshape(USERS), col_lse


def solution(mesh):
    fine = Mesh(mesh.devices.reshape(SIZES), AXES)
    by_item = ("zh", "x", "c", "zl", "y")
    by_user = ("zl", "y")
    placed = (P(by_item, None), P(), P(), P(by_item), P(by_user, None), P(by_user))
    return jax.shard_map(
        on_device,
        mesh=fine,
        in_specs=placed,
        out_specs=(P(by_user), P(by_item)),
        check_vma=False,
    )
```

```python
import functools
import math

import jax
import jax.numpy as jnp
from jax import lax
from jax.experimental import pallas as pl
from jax.experimental.pallas import tpu as pltpu
from jax.sharding import Mesh
from jax.sharding import PartitionSpec as P

F32, BF16 = jnp.float32, jnp.bfloat16
AXES = ("zl", "y", "zh", "x", "c")
SIZES = (16, 4, 2, 4, 2)
ZC = ("zl", "zh", "c")
PLANE = ("y", "x", "c")
RING = 32
BLOCK = 64
USERS = 512
Y = 4
DEPTH = 512
PARTS = 4
ITEMS = PARTS * BLOCK
HALF = ITEMS // 2
SEGMENT = 256
EXTRA = 16
TEMP = 4.0 / math.sqrt(DEPTH)
LOG2E = 1.0 / math.log(2.0)
CHUNK = 32


def ring_index(z, c):
    z = z % RING
    return (z % 16 * 2 + z // 16) * 2 + c


def along(distance):
    return [
        (ring_index(z, c), ring_index(z + (distance if c == 0 else -distance), c))
        for z in range(RING)
        for c in range(2)
    ]


def across(distance):
    return [
        (ring_index(z, c), ring_index(z + (distance if c == 1 else -distance), 1 - c))
        for z in range(RING)
        for c in range(2)
    ]


def high_low(values):
    high = values.astype(BF16)
    return high, (values - high.astype(F32)).astype(BF16)


def score_kernel(first, last, base_ref, items_ref, *refs):
    mine_ref, other_ref, *refs = refs
    rows = SEGMENT + EXTRA
    segments = [(ref, y * rows) for y in range(Y) for ref in (mine_ref, other_ref)]
    past_ref = None if first else refs.pop(0)
    item_ref, row_ref, scores, weight, ids, top_item, sum_item = refs
    for half in range(2):
        start = half * (HALF + EXTRA) + HALF
        extra = items_ref[start : start + EXTRA, 0:256].astype(F32)
        row = (extra[0:1, 0:128] + extra[0:1, 128:256]) * (1.0 / TEMP)
        weight[HALF * half : HALF * (half + 1), :] = jnp.broadcast_to(row, (HALF, 128)).T
    spot = lax.broadcasted_iota(jnp.int32, (BLOCK, 128), 0)
    for part in range(PARTS):
        ids[part * BLOCK : (part + 1) * BLOCK, :] = (spot + base_ref[part]).astype(F32)

    chunks = [slice(g, g + CHUNK) for g in range(0, ITEMS, CHUNK)]
    tiles = [slice(k, k + 128) for k in range(0, SEGMENT, 128)]
    items = jnp.concatenate(
        [items_ref[0:HALF, :], items_ref[HALF + EXTRA : 2 * HALF + EXTRA, :]], axis=0
    )
    tops, positives = [], []
    for s, (users_ref, start) in enumerate(segments):
        raw = lax.dot_general(
            items,
            users_ref[start : start + SEGMENT, :],
            (((1,), (1,)), ((), ())),
            preferred_element_type=F32,
        )
        index_rows = users_ref[start + SEGMENT : start + rows, 0:SEGMENT].astype(F32)
        wanted = index_rows[0:1, :] * 256.0 + index_rows[1:2, :]
        top_s, positive_s = [], []
        for k in tiles:
            top, positive = None, None
            for g in chunks:
                piece = raw[g, k]
                scores[g, s * SEGMENT + k.start : s * SEGMENT + k.stop] = piece
                if s == 0 and k.start == 0:
                    top_item[g, :] = piece
                else:
                    top_item[g, :] = jnp.maximum(top_item[g, :], piece)
                logits = piece + weight[g, :]
                found = jnp.where(ids[g, :] == wanted[:, k], logits, 0.0)
                shape = (CHUNK // 8, 8, 128)
                part_top = jnp.max(logits.reshape(shape), axis=0)
                part_positive = jnp.sum(found.reshape(shape), axis=0)
                top = part_top if top is None else jnp.maximum(top, part_top)
                positive = part_positive if positive is None else positive + part_positive
            top_s.append(jnp.max(top, axis=0, keepdims=True))
            positive_s.append(jnp.sum(positive, axis=0, keepdims=True))
        tops.append(top_s)
        positives.append(positive_s)

    for g in chunks:
        top_item[g, :] = jnp.broadcast_to(
            jnp.max(top_item[g, :], axis=1, keepdims=True), (CHUNK, 128)
        )
    ready = []
    for s in range(len(segments)):
        for t, k in enumerate(tiles):
            place = slice(s * SEGMENT + k.start, s * SEGMENT + k.stop)
            top, positive = tops[s][t], positives[s][t]
            if not first:
                old_top = past_ref[0:1, place]
                top = jnp.maximum(old_top, top)
                positive = positive + past_ref[2:3, place]
            total = None
            for g in chunks:
                piece = scores[g, place]
                by_item = jnp.exp2((piece - top_item[g, :]) * (TEMP * LOG2E))
                if s == 0 and t == 0:
                    sum_item[g, :] = by_item
                else:
                    sum_item[g, :] = sum_item[g, :] + by_item
                by_user = jnp.exp2((piece + weight[g, :] - top) * (TEMP * LOG2E))
                part = jnp.sum(by_user.reshape(CHUNK // 8, 8, 128), axis=0)
                total = part if total is None else total + part
            total = jnp.sum(total, axis=0, keepdims=True)
            if not first:
                total = total + past_ref[1:2, place] * jnp.exp2((old_top - top) * (TEMP * LOG2E))
            if last:
                lse = top * TEMP + jnp.log(total)
                ready.append((lse, positive * TEMP))
            else:
                row_ref[0:1, place] = top
                row_ref[1:2, place] = total
                row_ref[2:3, place] = positive
    if last:
        for y in range(Y):
            straight = ready[4 * y : 4 * y + 4]
            turned = straight[2:] + straight[:2]
            tile = jnp.concatenate(
                [
                    jnp.where(base_ref[PARTS] == 0, straight[t][kind], turned[t][kind])
                    for kind in range(2)
                    for t in range(4)
                ],
                axis=0,
            )
            for peer in range(8):
                row_ref[(y * 8 + peer) * 8 : (y * 8 + peer + 1) * 8, :] = tile
    for half in range(2):
        g = slice(128 * half, 128 * half + 128)
        total = jnp.broadcast_to(jnp.sum(sum_item[g, :], axis=1, keepdims=True), (128, 128))
        lse = top_item[g, :] * TEMP + jnp.log(total)
        item_ref[0:1, g] = lse.T[0:1, :]


def score_call(first, last, bases, items, users, past):
    vmem = pl.BlockSpec(memory_space=pltpu.VMEM)
    operands = (bases, items, *users) + (() if first else (past,))
    row_shape = (32 * 8, 128) if last else (8, Y * USERS)
    return pl.pallas_call(
        functools.partial(score_kernel, first, last),
        out_shape=(
            jax.ShapeDtypeStruct((1, ITEMS), F32),
            jax.ShapeDtypeStruct(row_shape, F32),
        ),
        in_specs=[pl.BlockSpec(memory_space=pltpu.SMEM)] + [vmem] * (len(operands) - 1),
        out_specs=(vmem, vmem),
        scratch_shapes=[
            pltpu.VMEM((ITEMS, Y * USERS), F32),
            pltpu.VMEM((ITEMS, 128), F32),
            pltpu.VMEM((ITEMS, 128), F32),
            pltpu.VMEM((ITEMS, 128), F32),
            pltpu.VMEM((ITEMS, 128), F32),
        ],
        compiler_params=pltpu.CompilerParams(vmem_limit_bytes=12 * 1024 * 1024),
        cost_estimate=pl.CostEstimate(
            flops=2 * ITEMS * Y * USERS * DEPTH,
            bytes_accessed=4 * 1024 * 1024,
            transcendentals=2 * ITEMS * Y * USERS,
        ),
    )(*operands)


def stack_kernel(near_ref, far_ref, pair_ref):
    pair_ref[0 : HALF + EXTRA, :] = near_ref[...]
    pair_ref[HALF + EXTRA :, :] = far_ref[...]


def stack_call(near, far):
    vmem = pl.BlockSpec(memory_space=pltpu.VMEM)
    return pl.pallas_call(
        stack_kernel,
        out_shape=jax.ShapeDtypeStruct((2 * (HALF + EXTRA), DEPTH), BF16),
        in_specs=[vmem, vmem],
        out_specs=vmem,
        compiler_params=pltpu.CompilerParams(vmem_limit_bytes=4 * 1024 * 1024),
        cost_estimate=pl.CostEstimate(flops=60 * 10**9, bytes_accessed=600_000, transcendentals=0),
    )(near, far)


def join(*parts):
    top = functools.reduce(jnp.maximum, parts)
    return top + jnp.log(sum(jnp.exp(part - top) for part in parts))


def on_device(item_features, layer_one, layer_two, log_weight, user_vectors, positive_index):
    hidden = jax.nn.relu(
        jnp.dot(item_features, layer_one, preferred_element_type=F32)
    ).astype(BF16)
    embedded = jnp.dot(hidden, layer_two, preferred_element_type=F32).astype(BF16)
    weight_high, weight_low = high_low(log_weight)

    zl, y, zh, x, c = (lax.axis_index(name) for name in AXES)
    def rows(values, count):
        return jnp.pad(values[None, :], ((0, count - 1), (0, DEPTH - values.shape[0])))

    sent = jnp.concatenate(
        [embedded, rows(jnp.concatenate([weight_high, weight_low]), 8)], axis=0
    )
    came = lax.ppermute(sent, ZC, across(1))
    weights = jnp.concatenate(
        [weight_high, came[BLOCK, 0:BLOCK], weight_low, came[BLOCK, BLOCK : 2 * BLOCK]]
    )
    near = jnp.concatenate([embedded, came[0:BLOCK], rows(weights, EXTRA)], axis=0)

    high = (positive_index // 256).astype(BF16).reshape(2, 1, SEGMENT)
    low = (positive_index % 256).astype(BF16).reshape(2, 1, SEGMENT)
    index_rows = jnp.pad(
        jnp.concatenate([high, low], axis=1), ((0, 0), (0, EXTRA - 2), (0, DEPTH - SEGMENT))
    )
    own = jnp.concatenate([user_vectors.reshape(2, SEGMENT, DEPTH), index_rows], axis=1)
    half = lax.dynamic_index_in_dim(own, c, 0, keepdims=False)

    far = lax.ppermute(near, ZC, along(4))
    half, near = lax.optimization_barrier((half, near))
    mine = lax.all_to_all(jnp.tile(half, (Y, 1)), "y", 0, 0, tiled=True)
    pair = stack_call(near, far)
    two_on = lax.ppermute(pair, ZC, along(2))
    one_on = lax.ppermute(pair, ZC, along(1))
    three_on = lax.ppermute(two_on, ZC, along(1))
    mine, two_here = lax.optimization_barrier((mine, two_on))
    users = [mine, lax.ppermute(mine, "c", [(0, 1), (1, 0)])]
    groups = [pair, one_on, two_here, three_on]

    z = zh * 16 + zl

    def base(place, core):
        place = place % RING
        item = ((place // 16) * 4 + x) * 2 + core
        return (item * 64 + (place % 16) * 4 + y) * BLOCK

    way = jnp.where(c == 0, -1, 1)
    columns, past = [], None
    for step in range(4):
        bases = jnp.stack(
            [
                base(z + way * (step + more + cross), jnp.where(cross == 0, c, 1 - c))
                for more in (0, 4)
                for cross in (0, 1)
            ]
            + [c]
        ).astype(jnp.int32)
        column, past = score_call(step == 0, step == 3, bases, groups[step], users, past)
        columns.append(column)

    stacked = jnp.concatenate(columns, axis=0)
    plane = lax.all_to_all(past, PLANE, 0, 0, tiled=True).reshape(32, 8, 128)
    came4 = lax.ppermute(stacked[:, HALF:], ZC, along(-4))

    lse, positive = plane[:, :4], plane[:, 4:]
    top = jnp.max(lse, axis=0)
    lse = top + jnp.log(jnp.sum(jnp.exp(lse - top), axis=0))
    mine = jnp.concatenate([lse, jnp.sum(positive, axis=0)], axis=0)
    four = join(stacked[:, :HALF], came4)
    came2 = lax.ppermute(four[2:], ZC, along(-2))
    other = lax.ppermute(mine, "zh", [(0, 1), (1, 0)])
    came2, _ = lax.optimization_barrier((came2, mine))
    two = join(four[:2], came2)
    one_away = lax.ppermute(two[1, :BLOCK], ZC, along(-1))
    cross_one = lax.ppermute(two[0, BLOCK:], ZC, across(1))
    cross_two = lax.ppermute(two[1, BLOCK:], ZC, across(2))
    row_loss = join(mine[:4], other[:4]) - (mine[4:] + other[4:])
    one_away, row_loss = lax.optimization_barrier((one_away, row_loss))
    col_lse = join(two[0, :BLOCK], one_away, cross_one, cross_two)
    return row_loss.reshape(USERS), col_lse


def solution(mesh):
    fine = Mesh(mesh.devices.reshape(SIZES), AXES)
    by_item = ("zh", "x", "c", "zl", "y")
    by_user = ("zl", "y")
    placed = (P(by_item, None), P(), P(), P(by_item), P(by_user, None), P(by_user))
    return jax.shard_map(
        on_device,
        mesh=fine,
        in_specs=placed,
        out_specs=(P(by_user), P(by_item)),
        check_vma=False,
    )
```

```python
import functools
import math

import jax
import jax.numpy as jnp
from jax import lax
from jax.experimental import pallas as pl
from jax.experimental.pallas import tpu as pltpu
from jax.sharding import Mesh
from jax.sharding import PartitionSpec as P

F32, BF16 = jnp.float32, jnp.bfloat16
AXES = ("zl", "y", "zh", "x", "c")
SIZES = (16, 4, 2, 4, 2)
ZC = ("zl", "zh", "c")
PLANE = ("y", "x", "c")
RING = 32
BLOCK = 64
USERS = 512
Y = 4
DEPTH = 512
PARTS = 4
ITEMS = PARTS * BLOCK
HALF = ITEMS // 2
SEGMENT = 256
EXTRA = 16
TEMP = 4.0 / math.sqrt(DEPTH)
LN2 = math.log(2.0)
LOG2E = 1.0 / LN2
CALLS = ((0, 1, 2), (3,))
GROUPS = ((0, 1, 2, 3), (4, 5, 6, 7))
CHUNK = 32


def ring_index(z, c):
    z = z % RING
    return (z % 16 * 2 + z // 16) * 2 + c


def along(distance):
    return [
        (ring_index(z, c), ring_index(z + (distance if c == 0 else -distance), c))
        for z in range(RING)
        for c in range(2)
    ]


def across(distance):
    return [
        (ring_index(z, c), ring_index(z + (distance if c == 1 else -distance), 1 - c))
        for z in range(RING)
        for c in range(2)
    ]


def high_low(values):
    high = values.astype(BF16)
    return high, (values - high.astype(F32)).astype(BF16)


def score_kernel(first, last, count, base_ref, *refs):
    items_refs, (mine_ref, other_ref, *refs) = refs[:count], refs[count:]
    rows = SEGMENT + EXTRA
    segments = [(ref, y * rows) for y in range(Y) for ref in (mine_ref, other_ref)]
    past_ref = None if first else refs.pop(0)
    item_ref, row_ref, scores, weight, ids, top_item, sum_item = refs
    halves = [(ref, half * (HALF + EXTRA)) for ref in items_refs for half in range(2)]
    for half, (items_ref, start) in enumerate(halves):
        extra = items_ref[start + HALF : start + HALF + EXTRA, 0:256].astype(F32)
        row = (extra[0:1, 0:128] + extra[0:1, 128:256]) * LOG2E
        weight[HALF * half : HALF * (half + 1), :] = jnp.broadcast_to(row, (HALF, 128)).T
    spot = lax.broadcasted_iota(jnp.int32, (BLOCK, 128), 0)
    for part in range(PARTS * count):
        ids[part * BLOCK : (part + 1) * BLOCK, :] = (spot + base_ref[part]).astype(F32)

    chunks = [slice(g, g + CHUNK) for g in range(0, ITEMS * count, CHUNK)]
    shape = (CHUNK // 8, 8, 128)
    items = jnp.concatenate([ref[start : start + HALF, :] for ref, start in halves], axis=0)
    tops, positives = {}, {}
    tiles_of = [
        [s * SEGMENT + k for s in group for k in range(0, SEGMENT, 128)]
        for group in GROUPS
    ]
    for group, tiles in zip(GROUPS, tiles_of):
        wanted = {}
        for s in group:
            users_ref, start = segments[s]
            scores[:, s * SEGMENT : (s + 1) * SEGMENT] = lax.dot_general(
                items,
                users_ref[start : start + SEGMENT, :],
                (((1,), (1,)), ((), ())),
                preferred_element_type=F32,
            ) * (TEMP * LOG2E)
            index_rows = users_ref[start + SEGMENT : start + rows, 0:SEGMENT].astype(F32)
            spots = index_rows[0:1, :] * 256.0 + index_rows[1:2, :]
            for k in range(0, SEGMENT, 128):
                wanted[s * SEGMENT + k] = jnp.broadcast_to(spots[:, k : k + 128], (8, 128))
        for g in chunks:
            best, heavy, known = None, weight[g, :].reshape(shape), ids[g, :].reshape(shape)
            if group != GROUPS[0]:
                best = top_item[g, :].reshape(shape)
            for k in tiles:
                piece = scores[g, k : k + 128].reshape(shape)
                best = piece if best is None else jnp.maximum(best, piece)
                logits = piece + heavy
                top = jnp.max(logits, axis=0)
                positive = jnp.sum(jnp.where(known == wanted[k], logits, 0.0), axis=0)
                tops[k] = jnp.maximum(tops[k], top) if k in tops else top
                positives[k] = positives[k] + positive if k in positives else positive
            top_item[g, :] = best.reshape(CHUNK, 128)

    for g in chunks:
        top_item[g, :] = jnp.broadcast_to(
            jnp.max(top_item[g, :], axis=1, keepdims=True), (CHUNK, 128)
        )
    ready = []
    for group, tiles in zip(GROUPS, tiles_of):
        level, totals = {}, {}
        for k in tiles:
            level[k] = jnp.max(tops[k], axis=0, keepdims=True)
            if not first:
                level[k] = jnp.maximum(past_ref[0:1, k : k + 128], level[k])
            level[k] = jnp.broadcast_to(level[k], (8, 128))
        for g in chunks:
            best, heavy = top_item[g, :].reshape(shape), weight[g, :].reshape(shape)
            amount = None if group == GROUPS[0] else sum_item[g, :].reshape(shape)
            for k in tiles:
                piece = scores[g, k : k + 128].reshape(shape)
                by_item = jnp.exp2(piece - best)
                amount = by_item if amount is None else amount + by_item
                part = jnp.sum(jnp.exp2(piece + heavy - level[k]), axis=0)
                totals[k] = totals[k] + part if k in totals else part
            sum_item[g, :] = amount.reshape(CHUNK, 128)
        for k in tiles:
            top = level[k][0:1, :]
            total = jnp.sum(totals[k], axis=0, keepdims=True)
            positive = jnp.sum(positives[k], axis=0, keepdims=True)
            if not first:
                total = total + past_ref[1:2, k : k + 128] * jnp.exp2(past_ref[0:1, k : k + 128] - top)
                positive = positive + past_ref[2:3, k : k + 128]
            if last:
                ready.append((top * LN2 + jnp.log(total), positive * LN2))
            else:
                row_ref[0:1, k : k + 128] = top
                row_ref[1:2, k : k + 128] = total
                row_ref[2:3, k : k + 128] = positive
    if last:
        for y in range(Y):
            straight = ready[4 * y : 4 * y + 4]
            turned = straight[2:] + straight[:2]
            tile = jnp.concatenate(
                [
                    jnp.where(base_ref[PARTS * count] == 0, straight[t][kind], turned[t][kind])
                    for kind in range(2)
                    for t in range(4)
                ],
                axis=0,
            )
            for peer in range(8):
                row_ref[(y * 8 + peer) * 8 : (y * 8 + peer + 1) * 8, :] = tile
    for half in range(2 * count):
        g = slice(128 * half, 128 * half + 128)
        total = jnp.broadcast_to(jnp.sum(sum_item[g, :], axis=1, keepdims=True), (128, 128))
        lse = top_item[g, :] * LN2 + jnp.log(total)
        item_ref[0:1, g] = lse.T[0:1, :]


def score_call(first, last, bases, items, users, past):
    vmem = pl.BlockSpec(memory_space=pltpu.VMEM)
    count = len(items)
    operands = (bases, *items, *users) + (() if first else (past,))
    row_shape = (32 * 8, 128) if last else (8, Y * USERS)
    return pl.pallas_call(
        functools.partial(score_kernel, first, last, count),
        out_shape=(
            jax.ShapeDtypeStruct((1, ITEMS * count), F32),
            jax.ShapeDtypeStruct(row_shape, F32),
        ),
        in_specs=[pl.BlockSpec(memory_space=pltpu.SMEM)] + [vmem] * (len(operands) - 1),
        out_specs=(vmem, vmem),
        scratch_shapes=[
            pltpu.VMEM((ITEMS * count, Y * USERS), F32),
            pltpu.VMEM((ITEMS * count, 128), F32),
            pltpu.VMEM((ITEMS * count, 128), F32),
            pltpu.VMEM((ITEMS * count, 128), F32),
            pltpu.VMEM((ITEMS * count, 128), F32),
        ],
        compiler_params=pltpu.CompilerParams(vmem_limit_bytes=20 * 1024 * 1024),
        cost_estimate=pl.CostEstimate(
            flops=2 * ITEMS * count * Y * USERS * DEPTH,
            bytes_accessed=4 * 1024 * 1024,
            transcendentals=2 * ITEMS * count * Y * USERS,
        ),
    )(*operands)


def stack_kernel(near_ref, far_ref, pair_ref):
    pair_ref[0 : HALF + EXTRA, :] = near_ref[...]
    pair_ref[HALF + EXTRA :, :] = far_ref[...]


def stack_call(near, far):
    vmem = pl.BlockSpec(memory_space=pltpu.VMEM)
    return pl.pallas_call(
        stack_kernel,
        out_shape=jax.ShapeDtypeStruct((2 * (HALF + EXTRA), DEPTH), BF16),
        in_specs=[vmem, vmem],
        out_specs=vmem,
        compiler_params=pltpu.CompilerParams(vmem_limit_bytes=4 * 1024 * 1024),
        cost_estimate=pl.CostEstimate(flops=60 * 10**9, bytes_accessed=600_000, transcendentals=0),
    )(near, far)


def join(*parts):
    top = functools.reduce(jnp.maximum, parts)
    return top + jnp.log(sum(jnp.exp(part - top) for part in parts))


def on_device(item_features, layer_one, layer_two, log_weight, user_vectors, positive_index):
    hidden = jax.nn.relu(
        jnp.dot(item_features, layer_one, preferred_element_type=F32)
    ).astype(BF16)
    embedded = jnp.dot(hidden, layer_two, preferred_element_type=F32).astype(BF16)
    weight_high, weight_low = high_low(log_weight)

    zl, y, zh, x, c = (lax.axis_index(name) for name in AXES)
    def rows(values, count):
        return jnp.pad(values[None, :], ((0, count - 1), (0, DEPTH - values.shape[0])))

    sent = jnp.concatenate(
        [embedded, rows(jnp.concatenate([weight_high, weight_low]), 8)], axis=0
    )
    came = lax.ppermute(sent, ZC, across(1))
    weights = jnp.concatenate(
        [weight_high, came[BLOCK, 0:BLOCK], weight_low, came[BLOCK, BLOCK : 2 * BLOCK]]
    )
    near = jnp.concatenate([embedded, came[0:BLOCK], rows(weights, EXTRA)], axis=0)

    high = (positive_index // 256).astype(BF16).reshape(2, 1, SEGMENT)
    low = (positive_index % 256).astype(BF16).reshape(2, 1, SEGMENT)
    index_rows = jnp.pad(
        jnp.concatenate([high, low], axis=1), ((0, 0), (0, EXTRA - 2), (0, DEPTH - SEGMENT))
    )
    own = jnp.concatenate([user_vectors.reshape(2, SEGMENT, DEPTH), index_rows], axis=1)
    half = lax.dynamic_index_in_dim(own, c, 0, keepdims=False)

    far = lax.ppermute(near, ZC, along(4))
    half, near = lax.optimization_barrier((half, near))
    mine = lax.all_to_all(jnp.tile(half, (Y, 1)), "y", 0, 0, tiled=True)
    pair = stack_call(near, far)
    two_on = lax.ppermute(pair, ZC, along(2))
    one_on = lax.ppermute(pair, ZC, along(1))
    one_on, two_on = lax.optimization_barrier((one_on, two_on))
    three_on = lax.ppermute(two_on, ZC, along(1))
    mine, two_here = lax.optimization_barrier((mine, two_on))
    users = [mine, lax.ppermute(mine, "c", [(0, 1), (1, 0)])]
    groups = [pair, one_on, two_here, three_on]

    z = zh * 16 + zl

    def base(place, core):
        place = place % RING
        item = ((place // 16) * 4 + x) * 2 + core
        return (item * 64 + (place % 16) * 4 + y) * BLOCK

    way = jnp.where(c == 0, -1, 1)
    columns, past = [], None
    for steps in CALLS:
        bases = jnp.stack(
            [
                base(z + way * (step + more + cross), jnp.where(cross == 0, c, 1 - c))
                for step in steps
                for more in (0, 4)
                for cross in (0, 1)
            ]
            + [c]
        ).astype(jnp.int32)
        column, past = score_call(
            steps[0] == 0, steps[-1] == 3, bases, [groups[step] for step in steps], users, past
        )
        columns.append(column.reshape(len(steps), ITEMS))

    stacked = jnp.concatenate(columns, axis=0)
    plane = lax.all_to_all(past, PLANE, 0, 0, tiled=True).reshape(32, 8, 128)
    came4 = lax.ppermute(stacked[:, HALF:], ZC, along(-4))

    lse, positive = plane[:, :4], plane[:, 4:]
    top = jnp.max(lse, axis=0)
    lse = top + jnp.log(jnp.sum(jnp.exp(lse - top), axis=0))
    mine = jnp.concatenate([lse, jnp.sum(positive, axis=0)], axis=0)
    four = join(stacked[:, :HALF], came4)
    came2 = lax.ppermute(four[2:], ZC, along(-2))
    other = lax.ppermute(mine, "zh", [(0, 1), (1, 0)])
    came2, _ = lax.optimization_barrier((came2, mine))
    two = join(four[:2], came2)
    one_away = lax.ppermute(two[1, :BLOCK], ZC, along(-1))
    cross_one = lax.ppermute(two[0, BLOCK:], ZC, across(1))
    cross_two = lax.ppermute(two[1, BLOCK:], ZC, across(2))
    row_loss = join(mine[:4], other[:4]) - (mine[4:] + other[4:])
    one_away, row_loss = lax.optimization_barrier((one_away, row_loss))
    col_lse = join(two[0, :BLOCK], one_away, cross_one, cross_two)
    return row_loss.reshape(USERS), col_lse


def solution(mesh):
    fine = Mesh(mesh.devices.reshape(SIZES), AXES)
    by_item = ("zh", "x", "c", "zl", "y")
    by_user = ("zl", "y")
    placed = (P(by_item, None), P(), P(), P(by_item), P(by_user, None), P(by_user))
    return jax.shard_map(
        on_device,
        mesh=fine,
        in_specs=placed,
        out_specs=(P(by_user), P(by_item)),
        check_vma=False,
    )
```

```python
import functools
import math

import jax
import jax.numpy as jnp
from jax import lax
from jax.experimental import pallas as pl
from jax.experimental.pallas import tpu as pltpu
from jax.sharding import Mesh
from jax.sharding import PartitionSpec as P

F32, BF16 = jnp.float32, jnp.bfloat16
AXES = ("zl", "y", "zh", "x", "c")
SIZES = (16, 4, 2, 4, 2)
ZC = ("zl", "zh", "c")
PLANE = ("y", "x", "c")
RING = 32
BLOCK = 64
USERS = 512
Y = 4
DEPTH = 512
PARTS = 4
ITEMS = PARTS * BLOCK
HALF = ITEMS // 2
SEGMENT = 256
EXTRA = 16
TEMP = 4.0 / math.sqrt(DEPTH)
LN2 = math.log(2.0)
LOG2E = 1.0 / LN2
GROUPS = ((0, 1, 2, 3), (4, 5, 6, 7))
CHUNK = 32


def ring_index(z, c):
    z = z % RING
    return (z % 16 * 2 + z // 16) * 2 + c


def along(distance):
    return [
        (ring_index(z, c), ring_index(z + (distance if c == 0 else -distance), c))
        for z in range(RING)
        for c in range(2)
    ]


def across(distance):
    return [
        (ring_index(z, c), ring_index(z + (distance if c == 1 else -distance), 1 - c))
        for z in range(RING)
        for c in range(2)
    ]


def high_low(values):
    high = values.astype(BF16)
    return high, (values - high.astype(F32)).astype(BF16)


def score_kernel(first, last, count, base_ref, *refs):
    items_ref, users_ref, *refs = refs
    segments = [(y * (USERS + EXTRA), k) for y in range(Y) for k in (0, SEGMENT)]
    past_ref = None if first else refs.pop(0)
    item_ref, row_ref, scores, weight, ids, top_item, sum_item = refs
    halves = [half * (HALF + EXTRA) for half in range(2 * count)]
    for half, start in enumerate(halves):
        extra = items_ref[start + HALF : start + HALF + EXTRA, 0:256].astype(F32)
        row = (extra[0:1, 0:128] + extra[0:1, 128:256]) * LOG2E
        weight[HALF * half : HALF * (half + 1), :] = jnp.broadcast_to(row, (HALF, 128)).T
    spot = lax.broadcasted_iota(jnp.int32, (BLOCK, 128), 0)
    for part in range(PARTS * count):
        ids[part * BLOCK : (part + 1) * BLOCK, :] = (spot + base_ref[part]).astype(F32)

    chunks = [slice(g, g + CHUNK) for g in range(0, ITEMS * count, CHUNK)]
    shape = (CHUNK // 8, 8, 128)
    items = jnp.concatenate([items_ref[start : start + HALF, :] for start in halves], axis=0)
    tops, positives = {}, {}
    tiles_of = [
        [s * SEGMENT + k for s in group for k in range(0, SEGMENT, 128)]
        for group in GROUPS
    ]
    for group, tiles in zip(GROUPS, tiles_of):
        wanted = {}
        for s in group:
            start, part = segments[s]
            scores[:, s * SEGMENT : (s + 1) * SEGMENT] = lax.dot_general(
                items,
                users_ref[start + part : start + part + SEGMENT, :],
                (((1,), (1,)), ((), ())),
                preferred_element_type=F32,
            ) * (TEMP * LOG2E)
            index_rows = users_ref[start + USERS : start + USERS + EXTRA, part : part + SEGMENT].astype(F32)
            spots = index_rows[0:1, :] * 256.0 + index_rows[1:2, :]
            for k in range(0, SEGMENT, 128):
                wanted[s * SEGMENT + k] = jnp.broadcast_to(spots[:, k : k + 128], (8, 128))
        for g in chunks:
            best, heavy, known = None, weight[g, :].reshape(shape), ids[g, :].reshape(shape)
            if group != GROUPS[0]:
                best = top_item[g, :].reshape(shape)
            for k in tiles:
                piece = scores[g, k : k + 128].reshape(shape)
                best = piece if best is None else jnp.maximum(best, piece)
                logits = piece + heavy
                top = jnp.max(logits, axis=0)
                positive = jnp.sum(jnp.where(known == wanted[k], logits, 0.0), axis=0)
                tops[k] = jnp.maximum(tops[k], top) if k in tops else top
                positives[k] = positives[k] + positive if k in positives else positive
            top_item[g, :] = best.reshape(CHUNK, 128)

    for g in chunks:
        top_item[g, :] = jnp.broadcast_to(
            jnp.max(top_item[g, :], axis=1, keepdims=True), (CHUNK, 128)
        )
    ready = []
    for group, tiles in zip(GROUPS, tiles_of):
        level, totals = {}, {}
        for k in tiles:
            level[k] = jnp.max(tops[k], axis=0, keepdims=True)
            if not first:
                level[k] = jnp.maximum(past_ref[0:1, k : k + 128], level[k])
            level[k] = jnp.broadcast_to(level[k], (8, 128))
        for g in chunks:
            best, heavy = top_item[g, :].reshape(shape), weight[g, :].reshape(shape)
            amount = None if group == GROUPS[0] else sum_item[g, :].reshape(shape)
            for k in tiles:
                piece = scores[g, k : k + 128].reshape(shape)
                by_item = jnp.exp2(piece - best)
                amount = by_item if amount is None else amount + by_item
                part = jnp.sum(jnp.exp2(piece + heavy - level[k]), axis=0)
                totals[k] = totals[k] + part if k in totals else part
            sum_item[g, :] = amount.reshape(CHUNK, 128)
        for k in tiles:
            top = level[k][0:1, :]
            total = jnp.sum(totals[k], axis=0, keepdims=True)
            positive = jnp.sum(positives[k], axis=0, keepdims=True)
            if not first:
                total = total + past_ref[1:2, k : k + 128] * jnp.exp2(past_ref[0:1, k : k + 128] - top)
                positive = positive + past_ref[2:3, k : k + 128]
            if last:
                ready.append((top * LN2 + jnp.log(total), positive * LN2))
            else:
                row_ref[0:1, k : k + 128] = top
                row_ref[1:2, k : k + 128] = total
                row_ref[2:3, k : k + 128] = positive
    if last:
        for y in range(Y):
            quarters = ready[4 * y : 4 * y + 4]
            tile = jnp.concatenate([lse for lse, _ in quarters] + [pos for _, pos in quarters], axis=0)
            for peer in range(8):
                row_ref[(y * 8 + peer) * 8 : (y * 8 + peer + 1) * 8, :] = tile
    for half in range(2 * count):
        g = slice(128 * half, 128 * half + 128)
        total = jnp.broadcast_to(jnp.sum(sum_item[g, :], axis=1, keepdims=True), (128, 128))
        lse = top_item[g, :] * LN2 + jnp.log(total)
        item_ref[0:1, g] = lse.T[0:1, :]


def score_call(first, last, count, bases, items, users, past):
    vmem = pl.BlockSpec(memory_space=pltpu.VMEM)
    operands = (bases, items, users) + (() if first else (past,))
    row_shape = (32 * 8, 128) if last else (8, Y * USERS)
    return pl.pallas_call(
        functools.partial(score_kernel, first, last, count),
        out_shape=(
            jax.ShapeDtypeStruct((1, ITEMS * count), F32),
            jax.ShapeDtypeStruct(row_shape, F32),
        ),
        in_specs=[pl.BlockSpec(memory_space=pltpu.SMEM)] + [vmem] * (len(operands) - 1),
        out_specs=(vmem, vmem),
        scratch_shapes=[
            pltpu.VMEM((ITEMS * count, Y * USERS), F32),
            pltpu.VMEM((ITEMS * count, 128), F32),
            pltpu.VMEM((ITEMS * count, 128), F32),
            pltpu.VMEM((ITEMS * count, 128), F32),
            pltpu.VMEM((ITEMS * count, 128), F32),
        ],
        compiler_params=pltpu.CompilerParams(vmem_limit_bytes=20 * 1024 * 1024),
        cost_estimate=pl.CostEstimate(
            flops=2 * ITEMS * count * Y * USERS * DEPTH,
            bytes_accessed=4 * 1024 * 1024,
            transcendentals=2 * ITEMS * count * Y * USERS,
        ),
    )(*operands)


def stack_kernel(first_ref, second_ref, both_ref):
    rows = first_ref.shape[0]
    both_ref[0:rows, :] = first_ref[...]
    both_ref[rows:, :] = second_ref[...]


def stack_call(first, second, flops):
    vmem = pl.BlockSpec(memory_space=pltpu.VMEM)
    return pl.pallas_call(
        stack_kernel,
        out_shape=jax.ShapeDtypeStruct((2 * first.shape[0], DEPTH), BF16),
        in_specs=[vmem, vmem],
        out_specs=vmem,
        compiler_params=pltpu.CompilerParams(vmem_limit_bytes=4 * 1024 * 1024),
        cost_estimate=pl.CostEstimate(flops=flops, bytes_accessed=600_000, transcendentals=0),
    )(first, second)


def join(*parts):
    top = functools.reduce(jnp.maximum, parts)
    return top + jnp.log(sum(jnp.exp(part - top) for part in parts))


def on_device(item_features, layer_one, layer_two, log_weight, user_vectors, positive_index):
    hidden = jax.nn.relu(
        jnp.dot(item_features, layer_one, preferred_element_type=F32)
    ).astype(BF16)
    embedded = jnp.dot(hidden, layer_two, preferred_element_type=F32).astype(BF16)
    weight_high, weight_low = high_low(log_weight)

    zl, y, zh, x, c = (lax.axis_index(name) for name in AXES)
    def rows(values, count):
        return jnp.pad(values[None, :], ((0, count - 1), (0, DEPTH - values.shape[0])))

    sent = jnp.concatenate(
        [embedded, rows(jnp.concatenate([weight_high, weight_low]), 8)], axis=0
    )
    came = lax.ppermute(sent, ZC, across(1))
    weights = jnp.concatenate(
        [weight_high, came[BLOCK, 0:BLOCK], weight_low, came[BLOCK, BLOCK : 2 * BLOCK]]
    )
    near = jnp.concatenate([embedded, came[0:BLOCK], rows(weights, EXTRA)], axis=0)

    high = (positive_index // 256).astype(BF16)
    low = (positive_index % 256).astype(BF16)
    index_rows = jnp.pad(jnp.stack([high, low]), ((0, EXTRA - 2), (0, 0)))
    own = jnp.concatenate([user_vectors, index_rows], axis=0)

    far = lax.ppermute(near, ZC, along(4))
    own, near = lax.optimization_barrier((own, near))
    users = lax.all_to_all(jnp.tile(own, (Y, 1)), "y", 0, 0, tiled=True)
    pair = stack_call(near, far, 60 * 10**9)
    evens = stack_call(pair, lax.ppermute(pair, ZC, along(2)), 10**6)
    odds = lax.ppermute(evens, ZC, along(1))

    z = zh * 16 + zl

    def base(place, core):
        place = place % RING
        item = ((place // 16) * 4 + x) * 2 + core
        return (item * 64 + (place % 16) * 4 + y) * BLOCK

    way = jnp.where(c == 0, -1, 1)
    columns, past = [], None
    for steps, items in (((0, 2), evens), ((1, 3), odds)):
        bases = jnp.stack(
            [
                base(z + way * (step + more + cross), jnp.where(cross == 0, c, 1 - c))
                for step in steps
                for more in (0, 4)
                for cross in (0, 1)
            ]
        ).astype(jnp.int32)
        column, past = score_call(steps[0] == 0, steps[-1] == 3, 2, bases, items, users, past)
        columns.append(column)

    stacked = jnp.stack([column[0, k : k + ITEMS] for k in (0, ITEMS) for column in columns])
    plane = lax.all_to_all(past, PLANE, 0, 0, tiled=True).reshape(32, 8, 128)
    came4 = lax.ppermute(stacked[:, HALF:], ZC, along(-4))

    lse, positive = plane[:, :4], plane[:, 4:]
    top = jnp.max(lse, axis=0)
    lse = top + jnp.log(jnp.sum(jnp.exp(lse - top), axis=0))
    mine = jnp.concatenate([lse, jnp.sum(positive, axis=0)], axis=0)
    four = join(stacked[:, :HALF], came4)
    came2 = lax.ppermute(four[2:], ZC, along(-2))
    other = lax.ppermute(mine, "zh", [(0, 1), (1, 0)])
    came2, _ = lax.optimization_barrier((came2, mine))
    two = join(four[:2], came2)
    one_away = lax.ppermute(two[1, :BLOCK], ZC, along(-1))
    cross_one = lax.ppermute(two[0, BLOCK:], ZC, across(1))
    cross_two = lax.ppermute(two[1, BLOCK:], ZC, across(2))
    row_loss = join(mine[:4], other[:4]) - (mine[4:] + other[4:])
    one_away, row_loss = lax.optimization_barrier((one_away, row_loss))
    col_lse = join(two[0, :BLOCK], one_away, cross_one, cross_two)
    return row_loss.reshape(USERS), col_lse


def solution(mesh):
    fine = Mesh(mesh.devices.reshape(SIZES), AXES)
    by_item = ("zh", "x", "c", "zl", "y")
    by_user = ("zl", "y")
    placed = (P(by_item, None), P(), P(), P(by_item), P(by_user, None), P(by_user))
    return jax.shard_map(
        on_device,
        mesh=fine,
        in_specs=placed,
        out_specs=(P(by_user), P(by_item)),
        check_vma=False,
    )
```

```python
import functools
import math

import jax
import jax.numpy as jnp
from jax import lax
from jax.experimental import pallas as pl
from jax.experimental.pallas import tpu as pltpu
from jax.sharding import Mesh
from jax.sharding import PartitionSpec as P

F32, BF16 = jnp.float32, jnp.bfloat16
AXES = ("zl", "y", "zh", "x", "c")
SIZES = (16, 4, 2, 4, 2)
ZC = ("zl", "zh", "c")
PLANE = ("y", "x", "c")
RING = 32
BLOCK = 64
USERS = 512
Y = 4
DEPTH = 512
PARTS = 4
ITEMS = PARTS * BLOCK
HALF = ITEMS // 2
SEGMENT = 256
EXTRA = 16
TEMP = 4.0 / math.sqrt(DEPTH)
LN2 = math.log(2.0)
LOG2E = 1.0 / LN2
GROUPS = ((0, 1, 2, 3), (4, 5, 6, 7))
CHUNK = 32


def ring_index(z, c):
    z = z % RING
    return (z % 16 * 2 + z // 16) * 2 + c


def along(distance):
    return [
        (ring_index(z, c), ring_index(z + (distance if c == 0 else -distance), c))
        for z in range(RING)
        for c in range(2)
    ]


def across(distance):
    return [
        (ring_index(z, c), ring_index(z + (distance if c == 1 else -distance), 1 - c))
        for z in range(RING)
        for c in range(2)
    ]


def high_low(values):
    high = values.astype(BF16)
    return high, (values - high.astype(F32)).astype(BF16)


def score_kernel(first, last, count, base_ref, *refs):
    items_ref, users_ref, *refs = refs
    segments = [(y * (USERS + EXTRA), k) for y in range(Y) for k in (0, SEGMENT)]
    past_ref = None if first else refs.pop(0)
    item_ref, row_ref, scores, weight, ids, top_item, sum_item = refs
    halves = [half * (HALF + EXTRA) for half in range(2 * count)]
    for half, start in enumerate(halves):
        extra = items_ref[start + HALF : start + HALF + EXTRA, 0:256].astype(F32)
        row = (extra[0:1, 0:128] + extra[0:1, 128:256]) * LOG2E
        weight[HALF * half : HALF * (half + 1), :] = jnp.broadcast_to(row, (HALF, 128)).T
    spot = lax.broadcasted_iota(jnp.int32, (BLOCK, 128), 0)
    for part in range(PARTS * count):
        ids[part * BLOCK : (part + 1) * BLOCK, :] = (spot + base_ref[part]).astype(F32)

    chunks = [slice(g, g + CHUNK) for g in range(0, ITEMS * count, CHUNK)]
    shape = (CHUNK // 8, 8, 128)
    items = jnp.concatenate([items_ref[start : start + HALF, :] for start in halves], axis=0)
    tops, positives = {}, {}
    tiles_of = [
        [s * SEGMENT + k for s in group for k in range(0, SEGMENT, 128)]
        for group in GROUPS
    ]
    for group, tiles in zip(GROUPS, tiles_of):
        wanted = {}
        for s in group:
            start, part = segments[s]
            scores[:, s * SEGMENT : (s + 1) * SEGMENT] = lax.dot_general(
                items,
                users_ref[start + part : start + part + SEGMENT, :],
                (((1,), (1,)), ((), ())),
                preferred_element_type=F32,
            ) * (TEMP * LOG2E)
            index_rows = users_ref[start + USERS : start + USERS + EXTRA, part : part + SEGMENT].astype(F32)
            spots = index_rows[0:1, :] * 256.0 + index_rows[1:2, :]
            for k in range(0, SEGMENT, 128):
                wanted[s * SEGMENT + k] = jnp.broadcast_to(spots[:, k : k + 128], (8, 128))
        for g in chunks:
            best, heavy, known = None, weight[g, :].reshape(shape), ids[g, :].reshape(shape)
            if group != GROUPS[0]:
                best = top_item[g, :].reshape(shape)
            for k in tiles:
                piece = scores[g, k : k + 128].reshape(shape)
                best = piece if best is None else jnp.maximum(best, piece)
                logits = piece + heavy
                top = jnp.max(logits, axis=0)
                positive = jnp.sum(jnp.where(known == wanted[k], logits, 0.0), axis=0)
                tops[k] = jnp.maximum(tops[k], top) if k in tops else top
                positives[k] = positives[k] + positive if k in positives else positive
            top_item[g, :] = best.reshape(CHUNK, 128)

    for g in chunks:
        top_item[g, :] = jnp.broadcast_to(
            jnp.max(top_item[g, :], axis=1, keepdims=True), (CHUNK, 128)
        )
    ready = []
    for group, tiles in zip(GROUPS, tiles_of):
        level, totals = {}, {}
        for k in tiles:
            level[k] = jnp.max(tops[k], axis=0, keepdims=True)
            if not first:
                level[k] = jnp.maximum(past_ref[0:1, k : k + 128], level[k])
            level[k] = jnp.broadcast_to(level[k], (8, 128))
        for g in chunks:
            best, heavy = top_item[g, :].reshape(shape), weight[g, :].reshape(shape)
            amount = None if group == GROUPS[0] else sum_item[g, :].reshape(shape)
            for k in tiles:
                piece = scores[g, k : k + 128].reshape(shape)
                by_item = jnp.exp2(piece - best)
                amount = by_item if amount is None else amount + by_item
                part = jnp.sum(jnp.exp2(piece + heavy - level[k]), axis=0)
                totals[k] = totals[k] + part if k in totals else part
            sum_item[g, :] = amount.reshape(CHUNK, 128)
        for k in tiles:
            top = level[k][0:1, :]
            total = jnp.sum(totals[k], axis=0, keepdims=True)
            positive = jnp.sum(positives[k], axis=0, keepdims=True)
            if not first:
                total = total + past_ref[1:2, k : k + 128] * jnp.exp2(past_ref[0:1, k : k + 128] - top)
                positive = positive + past_ref[2:3, k : k + 128]
            if last:
                ready.append((top * LN2 + jnp.log(total), positive * LN2))
            else:
                row_ref[0:1, k : k + 128] = top
                row_ref[1:2, k : k + 128] = total
                row_ref[2:3, k : k + 128] = positive
    if last:
        for y in range(Y):
            quarters = ready[4 * y : 4 * y + 4]
            tile = jnp.concatenate([lse for lse, _ in quarters] + [pos for _, pos in quarters], axis=0)
            for peer in range(8):
                row_ref[(y * 8 + peer) * 8 : (y * 8 + peer + 1) * 8, :] = tile
    for half in range(2 * count):
        g = slice(128 * half, 128 * half + 128)
        total = jnp.broadcast_to(jnp.sum(sum_item[g, :], axis=1, keepdims=True), (128, 128))
        lse = top_item[g, :] * LN2 + jnp.log(total)
        item_ref[0:1, g] = lse.T[0:1, :]


def score_call(first, last, count, bases, items, users, past):
    vmem = pl.BlockSpec(memory_space=pltpu.VMEM)
    operands = (bases, items, users) + (() if first else (past,))
    row_shape = (32 * 8, 128) if last else (8, Y * USERS)
    return pl.pallas_call(
        functools.partial(score_kernel, first, last, count),
        out_shape=(
            jax.ShapeDtypeStruct((1, ITEMS * count), F32),
            jax.ShapeDtypeStruct(row_shape, F32),
        ),
        in_specs=[pl.BlockSpec(memory_space=pltpu.SMEM)] + [vmem] * (len(operands) - 1),
        out_specs=(vmem, vmem),
        scratch_shapes=[
            pltpu.VMEM((ITEMS * count, Y * USERS), F32),
            pltpu.VMEM((ITEMS * count, 128), F32),
            pltpu.VMEM((ITEMS * count, 128), F32),
            pltpu.VMEM((ITEMS * count, 128), F32),
            pltpu.VMEM((ITEMS * count, 128), F32),
        ],
        compiler_params=pltpu.CompilerParams(vmem_limit_bytes=20 * 1024 * 1024),
        cost_estimate=pl.CostEstimate(
            flops=2 * ITEMS * count * Y * USERS * DEPTH,
            bytes_accessed=4 * 1024 * 1024,
            transcendentals=2 * ITEMS * count * Y * USERS,
        ),
    )(*operands)


def stack_kernel(first_ref, second_ref, both_ref):
    rows = first_ref.shape[0]
    both_ref[0:rows, :] = first_ref[...]
    both_ref[rows:, :] = second_ref[...]


def stack_call(first, second, flops):
    vmem = pl.BlockSpec(memory_space=pltpu.VMEM)
    return pl.pallas_call(
        stack_kernel,
        out_shape=jax.ShapeDtypeStruct((2 * first.shape[0], DEPTH), BF16),
        in_specs=[vmem, vmem],
        out_specs=vmem,
        compiler_params=pltpu.CompilerParams(vmem_limit_bytes=4 * 1024 * 1024),
        cost_estimate=pl.CostEstimate(flops=flops, bytes_accessed=600_000, transcendentals=0),
    )(first, second)


def join(*parts):
    top = functools.reduce(jnp.maximum, parts)
    return top + jnp.log(sum(jnp.exp(part - top) for part in parts))


def on_device(item_features, layer_one, layer_two, log_weight, user_vectors, positive_index):
    hidden = jax.nn.relu(
        jnp.dot(item_features, layer_one, preferred_element_type=F32)
    ).astype(BF16)
    embedded = jnp.dot(hidden, layer_two, preferred_element_type=F32).astype(BF16)
    weight_high, weight_low = high_low(log_weight)

    zl, y, zh, x, c = (lax.axis_index(name) for name in AXES)
    def rows(values, count):
        return jnp.pad(values[None, :], ((0, count - 1), (0, DEPTH - values.shape[0])))

    sent = jnp.concatenate(
        [embedded, rows(jnp.concatenate([weight_high, weight_low]), 8)], axis=0
    )
    came = lax.ppermute(sent, ZC, across(1))
    weights = jnp.concatenate(
        [weight_high, came[BLOCK, 0:BLOCK], weight_low, came[BLOCK, BLOCK : 2 * BLOCK]]
    )
    near = jnp.concatenate([embedded, came[0:BLOCK], rows(weights, EXTRA)], axis=0)

    high = (positive_index // 256).astype(BF16)
    low = (positive_index % 256).astype(BF16)
    index_rows = jnp.pad(jnp.stack([high, low]), ((0, EXTRA - 2), (0, 0)))
    own = jnp.concatenate([user_vectors, index_rows], axis=0)

    far = lax.ppermute(near, ZC, along(4))
    own, near = lax.optimization_barrier((own, near))
    users = lax.all_to_all(jnp.tile(own, (Y, 1)), "y", 0, 0, tiled=True)
    pair = stack_call(near, far, 60 * 10**9)
    evens = stack_call(pair, lax.ppermute(pair, ZC, along(2)), 10**6)
    odds = lax.ppermute(evens, ZC, along(1))

    z = zh * 16 + zl

    def base(place, core):
        place = place % RING
        item = ((place // 16) * 4 + x) * 2 + core
        return (item * 64 + (place % 16) * 4 + y) * BLOCK

    way = jnp.where(c == 0, -1, 1)
    columns, past = [], None
    for steps, items in (((0, 2), evens), ((1, 3), odds)):
        bases = jnp.stack(
            [
                base(z + way * (step + more + cross), jnp.where(cross == 0, c, 1 - c))
                for step in steps
                for more in (0, 4)
                for cross in (0, 1)
            ]
        ).astype(jnp.int32)
        column, past = score_call(steps[0] == 0, steps[-1] == 3, 2, bases, items, users, past)
        columns.append(column)

    stacked = jnp.stack([column[0, k : k + ITEMS] for k in (0, ITEMS) for column in columns])
    plane = lax.all_to_all(past, PLANE, 0, 0, tiled=True).reshape(32, 8, 128)
    came4 = lax.ppermute(stacked[:, HALF:], ZC, along(-4))

    lse, positive = plane[:, :4], plane[:, 4:]
    top = jnp.max(lse, axis=0)
    lse = top + jnp.log(jnp.sum(jnp.exp(lse - top), axis=0))
    mine = jnp.concatenate([lse, jnp.sum(positive, axis=0)], axis=0)
    came4, mine = lax.optimization_barrier((came4, mine))
    four = join(stacked[:, :HALF], came4)
    other = lax.ppermute(mine, "zh", [(0, 1), (1, 0)])
    came2 = lax.ppermute(four[2:], ZC, along(-2))
    two = join(four[:2], came2)
    one_away = lax.ppermute(two[1, :BLOCK], ZC, along(-1))
    cross_one = lax.ppermute(two[0, BLOCK:], ZC, across(1))
    cross_two = lax.ppermute(two[1, BLOCK:], ZC, across(2))
    row_loss = join(mine[:4], other[:4]) - (mine[4:] + other[4:])
    one_away, row_loss = lax.optimization_barrier((one_away, row_loss))
    col_lse = join(two[0, :BLOCK], one_away, cross_one, cross_two)
    return row_loss.reshape(USERS), col_lse


def solution(mesh):
    fine = Mesh(mesh.devices.reshape(SIZES), AXES)
    by_item = ("zh", "x", "c", "zl", "y")
    by_user = ("zl", "y")
    placed = (P(by_item, None), P(), P(), P(by_item), P(by_user, None), P(by_user))
    return jax.shard_map(
        on_device,
        mesh=fine,
        in_specs=placed,
        out_specs=(P(by_user), P(by_item)),
        check_vma=False,
    )
```
